128 devices in a mesh: row: 8 (over x, y_lo), col: 4 (over z), dp: 4 (over y_hi, core).
Axes of the slice: x: 4, y: 4 (y_hi: 2, y_lo: 2; y = y_hi * 2 + y_lo), z: 4, core: 2. Of those that a mesh axis runs over, the one named last changes fastest.
Arguments:
- inputs: bfloat16 [4, 2048, 10240], P('dp', 'col', 'row'), may hold values from -0.06591797 to 0.06591797
- grad_out: bfloat16 [4, 2048, 10240], P('dp', 'row', 'col'), may hold values from -6 to 6
- weight: bfloat16 [10240, 10240], P('row', 'col'), may hold values from -0.078125 to 0.078125
Outputs:
- grad_in: bfloat16 [4, 2048, 10240], P('dp', 'col', 'row')
- grad_weight: bfloat16 [10240, 10240], P('row', 'col')
The draws below stay inside these ranges and needn't reach their ends.
All inputs are finite; a program needn't handle non-finite values.
Results may differ from the reference program's by a relative error of at most 0.001.
Values may be sent and summed in bfloat16 or wider, within the bound.
No kernel may reach another device: no remote copies, remote signals or barrier semaphores. Data moves between devices by JAX's collectives and lax.ppermute only.
A program may use at most 192 MiB of HBM per device.

```python
import jax
import jax.numpy as jnp

ATT_WIDTH = 10240
OUT_WIDTH = 10240
TOK_ROW = 256
TOKENS = 2048
REPLICAS = 4
N_ROW = 8
N_DP = 4


def strengthened(result, rng, source, target, parts, factor):
    def block_of(axis_at):
        return (jnp.arange(result.shape[axis_at]) // (result.shape[axis_at] // parts)).reshape((-1,) + (1,) * (result.ndim - 1 - axis_at))

    one_side = jax.random.permutation(rng, parts)[block_of(target)]
    far = (block_of(target) + parts // 2) % parts
    return jnp.where((block_of(source) == one_side) | (block_of(source) == far), factor * result, result)


def level_of(stream_key, extent, pieces, least, high):
    def one(dim, parts):
        heights = jax.random.uniform(jax.random.fold_in(jax.random.fold_in(stream_key, 6), dim), (parts,), jnp.float32, least / len(pieces), high / len(pieces))
        return jnp.repeat(jnp.exp(heights), extent[dim] // parts).reshape((-1,) + (1,) * (len(extent) - dim - 1))

    gain = one(*pieces[0])
    for cut in pieces[1:]:
        gain = gain * one(*cut)
    return gain


def bell_draw(key, extent, width, reach, pieces=(), kind=jnp.bfloat16):
    result = jax.random.normal(key, extent, jnp.float32) * width
    if len(pieces) > 0:
        result = level_of(key, extent, pieces, -0.22, 0.18) * result
    return jnp.clip(result, min=-reach, max=reach).astype(kind)


def bell_draw_with(rng, shape, width, most, shards, heavy, kind=jnp.bfloat16):
    drawn = width * jax.random.normal(rng, shape, jnp.float32)
    if shards:
        drawn = drawn * level_of(rng, shape, shards, -0.22, 0.18)
    return jnp.clip(strengthened(drawn, jax.random.fold_in(rng, 3), *heavy), -most, most).astype(kind)


def setup_inputs(seed: int = 0) -> dict:
    splits = jax.random.split(jax.random.key(seed), 4)
    inputs = bell_draw(splits[0], (REPLICAS, TOKENS, ATT_WIDTH), ((TOK_ROW * N_ROW * N_DP) ** -0.5), 0.06591797, ((0, 4), (1, 4), (2, 8)))
    grad_out = bell_draw(splits[1], (REPLICAS, TOKENS, OUT_WIDTH), 1.0, 6.0, ((0, 4), (1, 8), (2, 4)))
    weight = bell_draw_with(splits[2], (ATT_WIDTH, OUT_WIDTH), OUT_WIDTH ** -0.5, 0.078125, ((0, 8), (1, 4)), (1, 0, 8, 2.0))
    return {"inputs": inputs, "grad_out": grad_out, "weight": weight}


def reference(inputs, grad_out, weight):
    results = []
    for replica in range(REPLICAS):
        term = jnp.dot(grad_out[replica], weight.T, preferred_element_type=jnp.float32)
        results.append(term.astype(jnp.bfloat16))
    grad_in = jnp.stack(results, 0)
    flat_in = inputs.reshape(-1, ATT_WIDTH)
    flat_out = grad_out.reshape(-1, OUT_WIDTH)
    grad_weight = jnp.dot(flat_in.T, flat_out, preferred_element_type=jnp.float32).astype(jnp.bfloat16)
    return grad_in, grad_weight
```

```python
import functools

import jax
import jax.numpy as jnp
from jax import lax
from jax.experimental import pallas as pl
from jax.experimental.pallas import tpu as pltpu
from jax.sharding import PartitionSpec as P

X_UP = [(r, (r + 2) % 8) for r in range(8)]
X_DOWN = [(r, (r - 2) % 8) for r in range(8)]
Y_SWAP = [(r, r ^ 1) for r in range(8)]
Z_UP = [(c, (c + 1) % 4) for c in range(4)]
Z_DOWN = [(c, (c - 1) % 4) for c in range(4)]
CORE_SWAP = [(d, d ^ 1) for d in range(4)]
FAR_SWAP = [(d, d ^ 2) for d in range(4)]

WIDTHS = (1024, 1536)
F32, BF16 = jnp.float32, jnp.bfloat16
ANY = pl.BlockSpec(memory_space=pl.ANY)
VMEM = pl.BlockSpec(memory_space=pltpu.VMEM)
SMEM = pl.BlockSpec(memory_space=pltpu.SMEM)
HBM = pl.BlockSpec(memory_space=pltpu.HBM)
CHEAP = pl.CostEstimate(flops=1, bytes_accessed=1, transcendentals=0)
POWER = 15.0
TAIL = 16
STEP = 32


def call(kernel, outs, scratch=(), specs=(), out_specs=None, mib=24, aliases=None):
    return pl.pallas_call(
        kernel,
        in_specs=list(specs),
        out_specs=out_specs or [VMEM] * len(outs),
        out_shape=list(outs),
        scratch_shapes=list(scratch),
        input_output_aliases=aliases or {},
        compiler_params=pltpu.CompilerParams(vmem_limit_bytes=mib << 20),
        cost_estimate=CHEAP,
    )


def after(x, *deps):
    return lax.optimization_barrier((x, *deps))[0]


def encode(src, dst, lo=0):
    n, c = src.shape

    def top_of(i, m):
        v = jnp.abs(src[pl.ds(pl.multiple_of(i * STEP, STEP), STEP), :])
        return jnp.maximum(m, jnp.max(v.reshape(STEP // 8, 8, c), axis=0))

    top = jnp.max(lax.fori_loop(0, n // STEP, top_of, jnp.zeros((8, c), F32)), keepdims=True)
    e = jnp.ceil(jnp.log2(jnp.clip(top, 2.0**-118, 2.0**120)))
    scale = jnp.exp2(8.0 - e)

    @pl.loop(0, n // STEP)
    def _(i):
        rows = pl.ds(pl.multiple_of(i * STEP, STEP), STEP)
        v = src[rows, :] * scale
        v2 = v * v
        v4 = v2 * v2
        dst[rows, :] = ((v4 * v4) * v4 * (v2 * v)).astype(BF16)

    dst[n:, :] = jnp.broadcast_to(e, (TAIL, c)).astype(BF16)


def scale_of(msg):
    n = msg.shape[0] - TAIL
    return jnp.exp2(msg[n:, 0:128].astype(F32)[0:1, 0:1] - 8.0)


def decode(y, scale):
    y = y.astype(F32)
    r = jnp.exp2(jnp.log2(jnp.abs(y)) * (1.0 / POWER)) * scale
    r = jnp.where(y == 0.0, 0.0, r)
    return jnp.where(y < 0.0, -r, r)


def looped(n, body):
    @pl.loop(0, n // STEP)
    def _(i):
        body(pl.ds(pl.multiple_of(i * STEP, STEP), STEP))


def weight_dot(held, grads, out):
    out[...] = lax.dot_general(held[...], grads[...], (((0,), (0,)), ((), ())), preferred_element_type=F32)


def give_kernel(first, at, inputs, a, b, a_up, a_dn, far_lo, far_hi, b_up, b_dn, b_far, give, grads, held, in_sem, sems):
    x, y, core = at[0], at[1], at[2]
    rows, width = a.shape[0], grads.shape[1]
    cols = pl.ds(first, width)
    half = give.shape[0]
    fetch = pltpu.make_async_copy(
        inputs.at[:, pl.ds(pl.multiple_of((1 - core) * half, half), half)], held, in_sem
    )
    fetch.start()
    copies = []

    def put(src, d, e, offset):
        r = 2 * lax.rem(x + d, 4) + lax.rem(y + e, 2)
        start = pl.multiple_of(r * rows + offset, rows // 2)
        copy = pltpu.make_async_copy(src, grads.at[pl.ds(start, src.shape[0])], sems.at[len(copies)])
        copy.start()
        copies.append(copy)

    put(a.at[:, cols], 0, 0, 0)
    put(b.at[:, cols], 0, 1, 0)
    put(a_up.at[:, cols], 1, 0, 0)
    put(a_dn.at[:, cols], 3, 0, 0)
    put(far_lo.at[:, cols], 2, 0, 0)
    put(far_hi.at[:, cols], 2, 0, rows // 2)
    put(b_up.at[:, cols], 1, 1, 0)
    put(b_dn.at[:, cols], 3, 1, 0)
    put(b_far.at[:, cols], 2, 1, 0)
    fetch.wait()
    for copy in copies:
        copy.wait()
    weight_dot(held, grads, give)


def keep_kernel(at, inputs, grads, keep, held, in_sem):
    half = keep.shape[0]
    fetch = pltpu.make_async_copy(
        inputs.at[:, pl.ds(pl.multiple_of(at[2] * half, half), half)], held, in_sem
    )
    fetch.start()
    fetch.wait()
    weight_dot(held, grads, keep)


def pair_kernel(keep, got, msg, total):
    def add(rows):
        total[rows, :] = keep[rows, :] + got[rows, :]

    looped(keep.shape[0], add)
    encode(total, msg)


def decode_kernel(msg, out):
    s = scale_of(msg)

    def one(rows):
        out[rows, :] = decode(msg[rows, :], s)

    looped(out.shape[0], one)


def final_kernel(at, mine, got, out):
    s = scale_of(got)

    def add(rows):
        out[rows, :] = (mine[rows, :] + decode(got[rows, :], s)).astype(BF16)

    looped(out.shape[0], add)


def place_kernel(first, at, own, other, old, out, sems):
    half, width = own.shape
    copies = []
    for i, (src, which) in enumerate(((own, at[2]), (other, 1 - at[2]))):
        rows = pl.ds(pl.multiple_of(which * half, half), half)
        copies.append(pltpu.make_async_copy(src, out.at[rows, pl.ds(first, width)], sems.at[i]))
    for copy in copies:
        copy.start()
    for copy in copies:
        copy.wait()


def block_sums(at, weight, grads, blocks, bufs, held, sems, done):
    rows = bufs.shape[1]
    fetch = pltpu.make_async_copy(weight, held, sems.at[0])
    fetch.start()
    copies = []
    for i, (s, part) in enumerate(blocks):
        start = lax.rem(at[3] + s, 4) * (2 * rows) + part * rows
        tokens = pl.ds(pl.multiple_of(start, rows), rows)
        first = 0
        for g in grads:
            width = g.shape[1]
            copies.append(
                pltpu.make_async_copy(g.at[tokens], bufs.at[i, :, pl.ds(first, width)], sems.at[1 + len(copies)])
            )
            copies[-1].start()
            first += width
    fetch.wait()
    for i in range(len(blocks)):
        for copy in copies[i * len(grads) : (i + 1) * len(grads)]:
            copy.wait()
        done(i, lax.dot_general(bufs[i], held[...], (((1,), (0,)), ((), ())), preferred_element_type=F32))


def first_kernel(n, at, weight, *refs):
    grads, (up, dn, totals, bufs, held, sems) = refs[:n], refs[n:]

    def done(i, value):
        totals[i // 2, pl.ds(256 * (i % 2), 256), :] = value
        if i % 2:
            encode(totals.at[i // 2], (up, dn)[i // 2])

    block_sums(at, weight, grads, ((2, 0), (1, 1), (3, 0), (2, 1)), bufs, held, sems, done)


def rest_kernel(n, at, weight, *refs):
    grads, (up, dn, own, bufs, held, sems) = refs[:n], refs[n:]

    def done(i, value):
        (up, dn, own.at[pl.ds(0, 256)], own.at[pl.ds(256, 256)])[i][...] = value

    block_sums(at, weight, grads, ((1, 0), (3, 1), (0, 0), (0, 1)), bufs, held, sems, done)


def second_kernel(at, up, dn, from_dn, from_up, up_msg, dn_msg, total):
    for mine, msg, first, dst in ((up, from_dn, 0, up_msg), (dn, from_up, 256, dn_msg)):
        s = scale_of(msg)

        @pl.loop(0, 256 // STEP)
        def _(i):
            at = pl.multiple_of(i * STEP, STEP)
            rows = pl.ds(at, STEP)
            total[rows, :] = mine[rows, :] + decode(msg[pl.ds(first + at, STEP), :], s)

        encode(total, dst)


def last_kernel(own, from_dn, from_up, second_dn, second_up, out):
    s1, s2, s3, s4 = (scale_of(m) for m in (from_dn, from_up, second_dn, second_up))

    @pl.loop(0, 256 // STEP)
    def _(i):
        at = pl.multiple_of(i * STEP, STEP)
        lo, hi = pl.ds(at, STEP), pl.ds(256 + at, STEP)
        out[lo, :] = (own[lo, :] + (decode(second_dn[lo, :], s3) + decode(from_up[lo, :], s2))).astype(BF16)
        out[hi, :] = (own[hi, :] + (decode(from_dn[hi, :], s1) + decode(second_up[lo, :], s4))).astype(BF16)


def shape(*dims, dtype=F32):
    return jax.ShapeDtypeStruct(dims, dtype)


def local(inputs, grad_out, weight):
    row, col, dp = (lax.axis_index(n) for n in ("row", "col", "dp"))
    at = jnp.stack([row // 2, row % 2, dp % 2, col]).astype(jnp.int32)
    input_rep = lax.all_gather(inputs, "col", axis=1, tiled=True)[0]
    tokens, features = input_rep.shape
    outs = weight.shape[1]
    dma, dmas = pltpu.SemaphoreType.DMA, lambda n: pltpu.SemaphoreType.DMA((n,))

    a = grad_out[0]
    h = a.shape[0] // 2
    a_dn = lax.ppermute(a, "row", X_UP)
    a_up = lax.ppermute(a, "row", X_DOWN)
    b = lax.ppermute(a, "row", Y_SWAP)
    weight_t = weight.T
    far_lo = lax.ppermute(after(a_up, weight_t)[:h], "row", X_DOWN)
    far_hi = lax.ppermute(a_dn[h:], "row", X_UP)
    b_dn = lax.ppermute(b, "row", X_UP)
    b_up = lax.ppermute(b, "row", X_DOWN)
    b_far = lax.ppermute(jnp.concatenate([far_lo, far_hi], axis=0), "row", Y_SWAP)
    pieces = (a, b, a_up, a_dn, far_lo, far_hi, b_up, b_dn, b_far)

    spans, first = [], 0
    for width in WIDTHS:
        spans.append((first, width))
        first += width
    grads, sent, got = [], [], []

    def weight_chunk(j, at, middle=None):
        first, width = spans[j]
        half = features // 2
        held = pltpu.VMEM((tokens, half), BF16)
        give, g = call(
            functools.partial(give_kernel, first),
            [shape(half, width), shape(tokens, width, dtype=BF16)],
            [held, dma, dmas(9)],
            [SMEM] + [HBM] * 10,
        )(at, input_rep, *pieces)
        swapped = lax.ppermute(give, "dp", CORE_SWAP)
        middle = middle and middle(g, give)
        (keep,) = call(keep_kernel, [shape(half, width)], [held, dma], [SMEM, HBM, VMEM])(
            after(at, give if middle is None else middle[0]), input_rep, g
        )
        (msg,) = call(
            pair_kernel, [shape(half + TAIL, width, dtype=BF16)], [pltpu.VMEM((half, width), F32)], [VMEM] * 2
        )(keep, swapped)
        grads.append(g)
        sent.append(msg)
        got.append(lax.ppermute(msg, "dp", FAR_SWAP))
        return middle

    n = len(spans)
    scratch = [pltpu.VMEM((4, 256, outs), BF16), pltpu.VMEM((outs, features), BF16), dmas(1 + 4 * n)]
    msg = shape(512 + TAIL, features, dtype=BF16)

    def send_terms(g, give):
        return call(
            functools.partial(first_kernel, n),
            [msg, msg],
            [pltpu.VMEM((2, 512, features), F32)] + scratch,
            [SMEM] + [HBM] * (n + 1),
            mib=28,
        )(after(at, give), weight_t, grads[0], g)

    weight_chunk(0, at)
    up_msg, dn_msg = weight_chunk(1, after(at, sent[0]), send_terms)
    from_dn = lax.ppermute(up_msg, "col", Z_UP)
    from_up = lax.ppermute(dn_msg, "col", Z_DOWN)
    up, dn, own = call(
        functools.partial(rest_kernel, n),
        [shape(256, features), shape(256, features), shape(512, features)],
        scratch,
        [SMEM] + [HBM] * (n + 1),
        mib=28,
    )(after(at, sent[1]), weight_t, *grads)
    msg = shape(256 + TAIL, features, dtype=BF16)

    half = features // 2

    def finish(j, at, grad_weight=None):
        first, width = spans[j]
        (mine,) = call(decode_kernel, [shape(half, width)], (), [VMEM])(sent[j])
        (total,) = call(final_kernel, [shape(half, width, dtype=BF16)], (), [SMEM] + [VMEM] * 2)(at, mine, got[j])
        other = lax.ppermute(total, "dp", CORE_SWAP)
        old = () if grad_weight is None else (grad_weight,)
        kernel = functools.partial(place_kernel, first)
        if not old:
            kernel = lambda at, own, other, out, sems, k=kernel: k(at, own, other, None, out, sems)
        (grad_weight,) = call(
            kernel,
            [shape(features, outs, dtype=BF16)],
            [dmas(2)],
            [SMEM, ANY, ANY] + [ANY] * len(old),
            [ANY],
            aliases={3: 0} if old else None,
        )(at, total, other, *old)
        return total, grad_weight

    total, grad_weight = finish(0, after(at, sent[1]))
    msg = shape(256 + TAIL, features, dtype=BF16)
    up_msg, dn_msg = call(second_kernel, [msg, msg], [pltpu.VMEM((256, features), F32)], [SMEM] + [VMEM] * 4)(
        after(at, total), up, dn, from_dn, from_up
    )
    second_dn = lax.ppermute(up_msg, "col", Z_UP)
    second_up = lax.ppermute(dn_msg, "col", Z_DOWN)
    (grad_in,) = call(last_kernel, [shape(512, features, dtype=BF16)], (), [VMEM] * 5)(
        own, from_dn, from_up, second_dn, second_up
    )
    _, grad_weight = finish(1, after(at, grad_in), grad_weight)
    return (grad_in[None], grad_weight)


def solution(mesh):
    in_specs = (P("dp", "col", "row"), P("dp", "row", "col"), P("row", "col"))
    out_specs = (P("dp", "col", "row"), P("row", "col"))
    return jax.shard_map(local, mesh=mesh, in_specs=in_specs, out_specs=out_specs, check_vma=False)
```

```python
import functools

import jax
import jax.numpy as jnp
from jax import lax
from jax.experimental import pallas as pl
from jax.experimental.pallas import tpu as pltpu
from jax.sharding import PartitionSpec as P

X_UP = [(r, (r + 2) % 8) for r in range(8)]
X_DOWN = [(r, (r - 2) % 8) for r in range(8)]
Y_SWAP = [(r, r ^ 1) for r in range(8)]
Z_UP = [(c, (c + 1) % 4) for c in range(4)]
Z_DOWN = [(c, (c - 1) % 4) for c in range(4)]
CORE_SWAP = [(d, d ^ 1) for d in range(4)]
FAR_SWAP = [(d, d ^ 2) for d in range(4)]

WIDTHS = (1280, 1280)
F32, BF16 = jnp.float32, jnp.bfloat16
ANY = pl.BlockSpec(memory_space=pl.ANY)
VMEM = pl.BlockSpec(memory_space=pltpu.VMEM)
SMEM = pl.BlockSpec(memory_space=pltpu.SMEM)
POWER = 15.0
PARTS = (1, 4)
SCHEDULE = (
    ("A", 0), ("T", 0), ("K0", 6), ("M", 150), ("P0", 0), ("K1", 0),
    ("P1", 0), ("B", 0), ("F0", 0), ("S", 30), ("L", 0), ("F1", 0),
    ("X0", 0), ("Y1", 0), ("Z1", 0),
)
TAIL = 16
STEP = 32


def call(kernel, outs, scratch=(), specs=(), out_specs=None, mib=14, aliases=None, us=0):
    return pl.pallas_call(
        kernel,
        in_specs=list(specs),
        out_specs=out_specs or [VMEM] * len(outs),
        out_shape=list(outs),
        scratch_shapes=list(scratch),
        input_output_aliases=aliases or {},
        compiler_params=pltpu.CompilerParams(vmem_limit_bytes=mib << 20),
        cost_estimate=pl.CostEstimate(flops=1 + us * 10**9, bytes_accessed=1, transcendentals=0),
    )


def after(x, *deps):
    return lax.optimization_barrier((x, *deps))[0]


def encode(srcs, dst):
    c = dst.shape[1]
    m = jnp.zeros((8, c), F32)
    for src in srcs:

        def top_of(i, m, src=src):
            v = jnp.abs(src[pl.ds(pl.multiple_of(i * STEP, STEP), STEP), :])
            return jnp.maximum(m, jnp.max(v.reshape(STEP // 8, 8, c), axis=0))

        m = lax.fori_loop(0, src.shape[0] // STEP, top_of, m)
    e = jnp.ceil(jnp.log2(jnp.clip(jnp.max(m, keepdims=True), 2.0**-118, 2.0**120)))
    scale = jnp.exp2(8.0 - e)
    first = 0
    for src in srcs:

        @pl.loop(0, src.shape[0] // STEP)
        def _(i, src=src, first=first):
            at = pl.multiple_of(i * STEP, STEP)
            v = src[pl.ds(at, STEP), :] * scale
            v2 = v * v
            v4 = v2 * v2
            dst[pl.ds(first + at, STEP), :] = ((v4 * v4) * v4 * (v2 * v)).astype(BF16)

        first += src.shape[0]
    dst[first:, :] = jnp.broadcast_to(e, (TAIL, c)).astype(BF16)


def scale_of(msg):
    n = msg.shape[0] - TAIL
    return jnp.exp2(msg[n:, 0:128].astype(F32)[0:1, 0:1] - 8.0)


def decode(y, scale):
    y = y.astype(F32)
    r = jnp.exp2(jnp.log2(jnp.abs(y)) * (1.0 / POWER)) * scale
    r = jnp.where(y == 0.0, 0.0, r)
    return jnp.where(y < 0.0, -r, r)


def looped(n, body):
    @pl.loop(0, n // STEP)
    def _(i):
        body(pl.multiple_of(i * STEP, STEP))


def turn_kernel(at, *refs):
    pieces, (out, bufs, sems) = refs[:5], refs[5:]
    rows = pieces[0].shape[0]
    copies, first = [], 0
    for i, src in enumerate(pieces):
        copies.append(pltpu.make_async_copy(src, bufs.at[pl.ds(first, src.shape[0])], sems.at[i]))
        copies[-1].start()
        first += src.shape[0]
    for copy in copies:
        copy.wait()
    for d in range(4):
        for f in range(0, out.shape[0], 256):
            tokens = pl.ds(pl.multiple_of(lax.rem(at[3] + d, 4) * rows, rows), rows)
            out[f : f + 256, tokens] = bufs[d * rows : (d + 1) * rows, f : f + 256].T


def weight_kernel(first, parts, at, inputs, *refs):
    gives, keep = refs[10 : 10 + parts], refs[10 + parts]
    weight_parts(first, at, inputs, refs[:10], gives, keep, *refs[11 + parts :])


def weight_parts(first, at, inputs, pieces, gives, keep, held, grads, sems):
    x, y, core = at[0], at[1], at[2]
    rows, width = pieces[0].shape[0], grads.shape[1]
    half = keep.shape[0]
    copies = [pltpu.make_async_copy(inputs, held, sems.at[10])]
    copies[0].start()
    for i, src in enumerate(pieces):
        d, lo = ((0, 0), (1, 0), (2, 0), (2, rows // 2), (3, 0))[i % 5]
        r = 2 * lax.rem(x + d, 4) + lax.rem(y + i // 5, 2)
        start = pl.multiple_of(r * rows + lo, rows // 2)
        dst = grads.at[pl.ds(start, src.shape[0])]
        copies.append(pltpu.make_async_copy(src.at[:, pl.ds(first, width)], dst, sems.at[i]))
        copies[-1].start()
    for copy in copies:
        copy.wait()
    def dot(which):
        features = pl.ds(pl.multiple_of(which * half, half), half)
        return jnp.dot(held[features, :], grads[...], preferred_element_type=F32)

    value, n = dot(1 - core), gives[0].shape[0]
    for i, give in enumerate(gives):
        give[...] = value[i * n : (i + 1) * n]
    keep[...] = dot(core)


def pair_kernel(at, keep, *refs):
    gots, (msg, total) = refs[:-2], refs[-2:]
    n = gots[0].shape[0]
    for k, got in enumerate(gots):

        def add(i, k=k, got=got):
            rows = pl.ds(k * n + i, STEP)
            total[rows, :] = keep[rows, :] + got[pl.ds(i, STEP), :]

        looped(n, add)
    encode([total], msg)


def decode_kernel(msg, out):
    s = scale_of(msg)

    def one(i):
        out[pl.ds(i, STEP), :] = decode(msg[pl.ds(i, STEP), :], s)

    looped(out.shape[0], one)


def final_kernel(at, mine, got, *outs):
    s = scale_of(got)
    n = outs[0].shape[0]
    for k, out in enumerate(outs):

        def add(i, k=k, out=out):
            rows = pl.ds(k * n + i, STEP)
            out[pl.ds(i, STEP), :] = (mine[rows, :] + decode(got[rows, :], s)).astype(BF16)

        looped(n, add)


def place_kernel(spots, at, *refs):
    out, sems = refs[-2:]
    copies = []
    for src, (first, other) in zip(refs, spots):
        half, width = src.shape
        which = 1 - at[2] if other else at[2]
        rows = pl.ds(pl.multiple_of(which * half, half), half)
        copies.append(pltpu.make_async_copy(src, out.at[rows, pl.ds(first, width)], sems.at[len(copies)]))
        copies[-1].start()
    for copy in copies:
        copy.wait()


def gate_kernel(at, got, out):
    out[0] = at[0]


def term_kernel(at, weight, *refs):
    pieces, (up, dn, terms, bufs, held, sems) = refs[:5], refs[5:]
    rows = bufs.shape[1]
    fetch = pltpu.make_async_copy(weight, held, sems.at[5])
    fetch.start()
    copies = []
    for i, (piece, d, lo) in enumerate(zip(pieces, (0, 1, 2, 2, 3), (0, 0, 0, rows // 2, 0))):
        copy = pltpu.make_async_copy(piece, bufs.at[d, pl.ds(lo, piece.shape[0])], sems.at[i])
        copy.start()
        copies.append((copy, d))
    fetch.wait()
    for d in range(4):
        for copy, i in copies:
            if i == d:
                copy.wait()
        s = lax.rem(at[0] + d + 4 - at[3], 4)
        terms[s] = lax.dot_general(bufs[d], held[...], (((1,), (1,)), ((), ())), preferred_element_type=F32)
    h = terms.shape[1] // 2
    lo, hi = pl.ds(0, h), pl.ds(h, h)
    encode([terms.at[2, lo], terms.at[1, hi]], up)
    encode([terms.at[3, lo], terms.at[2, hi]], dn)


def meet(terms, from_dn, from_up, sums):
    h = terms.shape[1] // 2
    dn, up = scale_of(from_dn), scale_of(from_up)

    def add(i):
        lo, hi = pl.ds(i, STEP), pl.ds(h + i, STEP)
        sums[lo, :] = terms[1, lo, :] + decode(from_dn[lo, :], dn)
        sums[hi, :] = terms[3, hi, :] + decode(from_up[hi, :], up)
        sums[pl.ds(2 * h + i, STEP), :] = terms[0, lo, :] + decode(from_up[lo, :], up)
        sums[pl.ds(3 * h + i, STEP), :] = terms[0, hi, :] + decode(from_dn[hi, :], dn)

    looped(h, add)


def meet_kernel(at, terms, from_dn, from_up, sums):
    meet(terms, from_dn, from_up, sums)


def second_kernel(at, sums_a, terms, from_dn, from_up, up, dn, sums_b):
    meet(terms, from_dn, from_up, sums_b)
    h = sums_a.shape[0] // 4
    for first, msg in ((0, up), (h, dn)):
        encode([sums_a.at[pl.ds(first, h)], sums_b.at[pl.ds(first, h)]], msg)


def last_kernel(at, sums_a, sums_b, second_dn, second_up, out):
    dn, up = scale_of(second_dn), scale_of(second_up)
    h = sums_a.shape[0] // 4
    for k, sums in enumerate((sums_a, sums_b)):
        first = lax.rem(at[1] + k, 2) * (2 * h)

        def add(i):
            msg = pl.ds(k * h + i, STEP)
            a = sums[pl.ds(2 * h + i, STEP), :] + decode(second_dn[msg, :], dn)
            b = sums[pl.ds(3 * h + i, STEP), :] + decode(second_up[msg, :], up)
            out[pl.ds(pl.multiple_of(first + i, STEP), STEP), :] = a.astype(BF16)
            out[pl.ds(pl.multiple_of(first + h + i, STEP), STEP), :] = b.astype(BF16)

        looped(h, add)


def shape(*dims, dtype=F32):
    return jax.ShapeDtypeStruct(dims, dtype)


def local(inputs, grad_out, weight):
    row, col, dp = (lax.axis_index(n) for n in ("row", "col", "dp"))
    where = jnp.stack([row // 2, row % 2, dp % 2, col]).astype(jnp.int32)
    features, outs = weight.shape
    half = features // 2
    dmas = lambda n: pltpu.SemaphoreType.DMA((n,))

    a = grad_out[0]
    rows = a.shape[0]
    h = rows // 2
    a_dn = lax.ppermute(a, "row", X_UP)
    a_up = lax.ppermute(a, "row", X_DOWN)
    b = lax.ppermute(a, "row", Y_SWAP)
    i_dn = lax.ppermute(inputs[0], "col", Z_UP)
    i_up = lax.ppermute(inputs[0], "col", Z_DOWN)
    far_lo = lax.ppermute(a_up[:h], "row", X_DOWN)
    far_hi = lax.ppermute(a_dn[h:], "row", X_UP)
    b_dn = lax.ppermute(after(b, far_hi), "row", X_UP)
    b_up = lax.ppermute(after(b, far_lo), "row", X_DOWN)
    i_far_lo = lax.ppermute(i_up[:rows], "col", Z_DOWN)
    i_far_hi = lax.ppermute(i_dn[rows:], "col", Z_UP)
    b_far_lo = lax.ppermute(far_lo, "row", Y_SWAP)
    b_far_hi = lax.ppermute(far_hi, "row", Y_SWAP)
    side_a, side_b = (a, a_up, far_lo, far_hi, a_dn), (b, b_up, b_far_lo, b_far_hi, b_dn)
    input_pieces = (inputs[0], i_up, i_far_lo, i_far_hi, i_dn)
    tokens = 8 * rows

    spans, first = [], 0
    for width in WIDTHS:
        spans.append((first, width))
        first += width

    last = []

    def ordered(kernel, outs, scratch, specs, *args, **kw):
        results = call(kernel, outs, scratch, [SMEM] + specs, **kw)(after(where, *last), *args)
        last[:] = [results[0]]
        return results

    def terms_of(side, us=0):
        msg = shape(rows + TAIL, features, dtype=BF16)
        up, dn, terms = ordered(
            term_kernel,
            [msg, msg, shape(4, rows, features)],
            [pltpu.VMEM((4, rows, outs), BF16), pltpu.VMEM((features, outs), BF16), dmas(6)],
            [ANY] * 6,
            weight,
            *side,
            mib=22,
            us=us,
        )
        return terms, lax.ppermute(up, "col", Z_UP), lax.ppermute(dn, "col", Z_DOWN)

    def weight_of(j, us=0):
        first, width = spans[j]
        parts = PARTS[j]
        *gives, keep = ordered(
            functools.partial(weight_kernel, first, parts),
            [shape(half // parts, width)] * parts + [shape(half, width)],
            [pltpu.VMEM((features, tokens), BF16), pltpu.VMEM((tokens, width), BF16), dmas(11)],
            [ANY] * 11,
            env["T"],
            *side_a,
            *side_b,
            us=us,
            mib=20,
        )
        return [keep] + [lax.ppermute(give, "dp", CORE_SWAP) for give in gives]

    def pair_of(j, us=0):
        width = spans[j][1]
        parts = env["K%d" % j]
        (msg,) = ordered(
            pair_kernel,
            [shape(half + TAIL, width, dtype=BF16)],
            [pltpu.VMEM((half, width), F32)],
            [VMEM] * len(parts),
            *parts,
            us=us,
        )
        return msg, lax.ppermute(msg, "dp", FAR_SWAP)

    def final_of(j, us=0):
        width = spans[j][1]
        sent, got = env["P%d" % j]
        (mine,) = call(decode_kernel, [shape(half, width)], (), [VMEM])(sent)
        (own,) = ordered(final_kernel, [shape(half, width, dtype=BF16)], (), [VMEM] * 2, mine, got, us=us)
        return own, lax.ppermute(own, "dp", CORE_SWAP)

    def turn(us=0):
        (turned,) = ordered(
            turn_kernel,
            [shape(features, tokens, dtype=BF16)],
            [pltpu.VMEM((tokens, features), BF16), dmas(5)],
            [ANY] * 5,
            *input_pieces,
            us=us,
        )
        return turned

    def meet_of(us=0):
        (sums,) = ordered(meet_kernel, [shape(2 * rows, features)], (), [VMEM] * 3, *env["A"], us=us)
        return sums

    def second_of(us=0):
        msg = shape(rows + TAIL, features, dtype=BF16)
        up, dn, sums = ordered(
            second_kernel, [msg, msg, shape(2 * rows, features)], (), [VMEM] * 4, env["M"], *env["B"], mib=18, us=us
        )
        return sums, lax.ppermute(up, "col", Z_UP), lax.ppermute(dn, "col", Z_DOWN)

    def last_of(us=0):
        out = [shape(2 * rows, features, dtype=BF16)]
        (grad_in,) = ordered(last_kernel, out, (), [VMEM] * 4, env["M"], *env["S"], us=us)
        return grad_in

    def place(chunks, sides, us=0):
        old = [env["X"]] if "X" in env else []
        spots = [(j, i) for j in chunks for i in sides]
        n = len(spots)
        (out,) = ordered(
            functools.partial(place_kernel, [(spans[j][0], i) for j, i in spots]),
            [shape(features, outs, dtype=BF16)],
            [dmas(n)],
            [ANY] * (n + len(old)),
            *[env["F%d" % j][i] for j, i in spots],
            *old,
            out_specs=[ANY],
            aliases={n + 1: 0} if old else None,
            us=us,
        )
        return out

    def gate(j, us):
        ordered(gate_kernel, [shape(1, dtype=jnp.int32)], (), [ANY], env["P%d" % j][1], out_specs=[SMEM], us=us)

    env = {}
    for name, us in SCHEDULE:
        if name == "A":
            env[name] = terms_of(side_a, us)
        elif name == "B":
            env[name] = terms_of(side_b, us)
        elif name[0] in "XYZ":
            env["X"] = place([int(c) for c in name[1:]], {"X": (0, 1), "Y": (0,), "Z": (1,)}[name[0]], us)
        elif name[0] == "G":
            gate(int(name[1]), us)
        elif name[0] in "KPF":
            env[name] = {"K": weight_of, "P": pair_of, "F": final_of}[name[0]](int(name[1]), us)
        else:
            env[name] = {"T": turn, "M": meet_of, "S": second_of, "L": last_of}[name](us)
    grad_in, grad_weight = env["L"], env["X"]
    return (grad_in[None], grad_weight)


def solution(mesh):
    in_specs = (P("dp", "col", "row"), P("dp", "row", "col"), P("row", "col"))
    out_specs = (P("dp", "col", "row"), P("row", "col"))
    return jax.shard_map(local, mesh=mesh, in_specs=in_specs, out_specs=out_specs, check_vma=False)
```

```python
import functools

import jax
import jax.numpy as jnp
from jax import lax
from jax.experimental import pallas as pl
from jax.experimental.pallas import tpu as pltpu
from jax.sharding import PartitionSpec as P

X_UP = [(r, (r + 2) % 8) for r in range(8)]
X_DOWN = [(r, (r - 2) % 8) for r in range(8)]
Y_SWAP = [(r, r ^ 1) for r in range(8)]
Z_UP = [(c, (c + 1) % 4) for c in range(4)]
Z_DOWN = [(c, (c - 1) % 4) for c in range(4)]
CORE_SWAP = [(d, d ^ 1) for d in range(4)]
FAR_SWAP = [(d, d ^ 2) for d in range(4)]

WIDTHS = (1280, 1280)
F32, BF16 = jnp.float32, jnp.bfloat16
ANY = pl.BlockSpec(memory_space=pl.ANY)
VMEM = pl.BlockSpec(memory_space=pltpu.VMEM)
SMEM = pl.BlockSpec(memory_space=pltpu.SMEM)
POWER = 15.0
PARTS = (1, 2)
SCHEDULE = (
    ("A", 0), ("T", 0), ("K0", 6), ("M", 150), ("P0", 0), ("B", 0),
    ("K1", 0), ("P1", 0), ("F0", 0), ("S", 30), ("X0", 0), ("L", 0),
    ("F1", 0), ("Y1", 0), ("Z1", 0),
)
HALVES = (1, 1)
TAIL = 16
STEP = 32


def call(kernel, outs, scratch=(), specs=(), out_specs=None, mib=14, aliases=None, us=0):
    return pl.pallas_call(
        kernel,
        in_specs=list(specs),
        out_specs=out_specs or [VMEM] * len(outs),
        out_shape=list(outs),
        scratch_shapes=list(scratch),
        input_output_aliases=aliases or {},
        compiler_params=pltpu.CompilerParams(vmem_limit_bytes=mib << 20),
        cost_estimate=pl.CostEstimate(flops=1 + us * 10**9, bytes_accessed=1, transcendentals=0),
    )


def after(x, *deps):
    return lax.optimization_barrier((x, *deps))[0]


def encode(srcs, dst):
    c = dst.shape[1]
    m = jnp.zeros((8, c), F32)
    for src in srcs:

        def top_of(i, m, src=src):
            return top_with(m, src[pl.ds(pl.multiple_of(i * STEP, STEP), STEP), :])

        m = lax.fori_loop(0, src.shape[0] // STEP, top_of, m)
    encode_with(m, srcs, dst)


def top_with(m, v):
    return jnp.maximum(m, jnp.max(jnp.abs(v).reshape(STEP // 8, 8, v.shape[1]), axis=0))


def encode_with(m, srcs, dst):
    c = dst.shape[1]
    e = jnp.ceil(jnp.log2(jnp.clip(jnp.max(m, keepdims=True), 2.0**-118, 2.0**120)))
    scale = jnp.exp2(8.0 - e)
    first = 0
    for src in srcs:

        @pl.loop(0, src.shape[0] // STEP)
        def _(i, src=src, first=first):
            at = pl.multiple_of(i * STEP, STEP)
            v = src[pl.ds(at, STEP), :] * scale
            v2 = v * v
            v4 = v2 * v2
            dst[pl.ds(first + at, STEP), :] = ((v4 * v4) * v4 * (v2 * v)).astype(BF16)

        first += src.shape[0]
    dst[first:, :] = jnp.broadcast_to(e, (TAIL, c)).astype(BF16)


def scale_of(msg):
    n = msg.shape[0] - TAIL
    return jnp.exp2(msg[n:, 0:128].astype(F32)[0:1, 0:1] - 8.0)


def decode(y, scale):
    y = y.astype(F32)
    r = jnp.exp2(jnp.log2(jnp.abs(y)) * (1.0 / POWER)) * scale
    r = jnp.where(y == 0.0, 0.0, r)
    return jnp.where(y < 0.0, -r, r)


def looped(n, body):
    @pl.loop(0, n // STEP)
    def _(i):
        body(pl.multiple_of(i * STEP, STEP))


def turn_kernel(at, *refs):
    pieces, (out, bufs, sems) = refs[:-3], refs[-3:]
    rows = pieces[0].shape[0]
    copies, first = [], 0
    for i, src in enumerate(pieces):
        copies.append(pltpu.make_async_copy(src, bufs.at[pl.ds(first, src.shape[0])], sems.at[i]))
        copies[-1].start()
        first += src.shape[0]
    for copy in copies:
        copy.wait()
    for d in range(4):
        for f in range(0, out.shape[0], 256):
            tokens = pl.ds(pl.multiple_of(lax.rem(at[3] + d, 4) * rows, rows), rows)
            out[f : f + 256, tokens] = bufs[d * rows : (d + 1) * rows, f : f + 256].T


def weight_kernel(first, parts, own, at, inputs, *refs):
    n = 10 + parts + own
    weight_parts(first, at, inputs, refs[:10], refs[10 : 10 + parts], refs[10 + parts : n], *refs[n:])


def weight_parts(first, at, inputs, pieces, gives, keeps, grads, sems):
    x, y, core = at[0], at[1], at[2]
    rows, width = pieces[0].shape[0], grads.shape[1]
    half = inputs.shape[0] // 2
    cut = width // 2 // 256 * 256
    tiles = ((0, cut), (cut, width - cut))
    copies = []
    for t, (column, n) in enumerate(tiles):
        for i, src in enumerate(pieces):
            d, lo = ((0, 0), (1, 0), (2, 0), (2, rows // 2), (3, 0))[i % 5]
            r = 2 * lax.rem(x + d, 4) + lax.rem(y + i // 5, 2)
            start = pl.multiple_of(r * rows + lo, rows // 2)
            dst = grads.at[pl.ds(start, src.shape[0]), pl.ds(column, n)]
            copy = pltpu.make_async_copy(src.at[:, pl.ds(first + column, n)], dst, sems.at[10 * t + i])
            copy.start()
            copies.append(copy)
    wanted = [1 - core] * (len(gives) > 0) + [core] * len(keeps)
    for t, (column, n) in enumerate(tiles):
        for copy in copies[10 * t : 10 * t + 10]:
            copy.wait()
        columns = pl.ds(column, n)
        for i, which in enumerate(wanted):
            features = pl.ds(pl.multiple_of(which * half, half), half)
            value = jnp.dot(inputs[features, :], grads[:, columns], preferred_element_type=F32)
            if i == 0 and gives:
                m = gives[0].shape[0]
                for k, give in enumerate(gives):
                    give[:, columns] = value[k * m : (k + 1) * m]
            else:
                keeps[0][:, columns] = value


def pair_kernel(at, keep, *refs):
    gots, (msg, total) = refs[:-2], refs[-2:]
    n = gots[0].shape[0]
    m = jnp.zeros((8, total.shape[1]), F32)
    for k, got in enumerate(gots):

        def add(i, m, k=k, got=got):
            i = pl.multiple_of(i * STEP, STEP)
            rows = pl.ds(k * n + i, STEP)
            value = keep[rows, :] + got[pl.ds(i, STEP), :]
            total[rows, :] = value
            return top_with(m, value)

        m = lax.fori_loop(0, n // STEP, add, m)
    encode_with(m, [total], msg)


def decode_kernel(msg, out):
    s = scale_of(msg)

    def one(i):
        out[pl.ds(i, STEP), :] = decode(msg[pl.ds(i, STEP), :], s)

    looped(out.shape[0], one)


def final_kernel(first, at, mine, got, out):
    s = scale_of(got)

    def add(i):
        rows = pl.ds(first + i, STEP)
        out[pl.ds(i, STEP), :] = (mine[rows, :] + decode(got[rows, :], s)).astype(BF16)

    looped(out.shape[0], add)


def place_kernel(spots, at, *refs):
    out, sems = refs[-2:]
    half = out.shape[0] // 2
    copies = []
    for src, (column, row, other) in zip(refs, spots):
        n, width = src.shape
        which = 1 - at[2] if other else at[2]
        rows = pl.ds(pl.multiple_of(which * half + row, n), n)
        copies.append(pltpu.make_async_copy(src, out.at[rows, pl.ds(column, width)], sems.at[len(copies)]))
        copies[-1].start()
    for copy in copies:
        copy.wait()


def gate_kernel(at, got, out):
    out[0] = at[0]


def term_kernel(at, weight, *refs):
    pieces, (up, dn, terms, bufs, held, sems) = refs[:5], refs[5:]
    rows = bufs.shape[1]
    fetch = pltpu.make_async_copy(weight, held, sems.at[5])
    fetch.start()
    copies = []
    for i, (piece, d, lo) in enumerate(zip(pieces, (0, 1, 2, 2, 3), (0, 0, 0, rows // 2, 0))):
        copy = pltpu.make_async_copy(piece, bufs.at[d, pl.ds(lo, piece.shape[0])], sems.at[i])
        copy.start()
        copies.append((copy, d))
    fetch.wait()
    for d in range(4):
        for copy, i in copies:
            if i == d:
                copy.wait()
        s = lax.rem(at[0] + d + 4 - at[3], 4)
        terms[s] = lax.dot_general(bufs[d], held[...], (((1,), (1,)), ((), ())), preferred_element_type=F32)
    h = terms.shape[1] // 2
    lo, hi = pl.ds(0, h), pl.ds(h, h)
    encode([terms.at[2, lo], terms.at[1, hi]], up)
    encode([terms.at[3, lo], terms.at[2, hi]], dn)


def meet(terms, from_dn, from_up, sums):
    h = terms.shape[1] // 2
    dn, up = scale_of(from_dn), scale_of(from_up)

    def add(i):
        lo, hi = pl.ds(i, STEP), pl.ds(h + i, STEP)
        sums[lo, :] = terms[1, lo, :] + decode(from_dn[lo, :], dn)
        sums[hi, :] = terms[3, hi, :] + decode(from_up[hi, :], up)
        sums[pl.ds(2 * h + i, STEP), :] = terms[0, lo, :] + decode(from_up[lo, :], up)
        sums[pl.ds(3 * h + i, STEP), :] = terms[0, hi, :] + decode(from_dn[hi, :], dn)

    looped(h, add)


def meet_kernel(at, terms, from_dn, from_up, sums):
    meet(terms, from_dn, from_up, sums)


def second_kernel(at, sums_a, terms, from_dn, from_up, up, dn, sums_b):
    meet(terms, from_dn, from_up, sums_b)
    h = sums_a.shape[0] // 4
    for first, msg in ((0, up), (h, dn)):
        encode([sums_a.at[pl.ds(first, h)], sums_b.at[pl.ds(first, h)]], msg)


def last_kernel(at, sums_a, sums_b, second_dn, second_up, out):
    dn, up = scale_of(second_dn), scale_of(second_up)
    h = sums_a.shape[0] // 4
    for k, sums in enumerate((sums_a, sums_b)):
        first = lax.rem(at[1] + k, 2) * (2 * h)

        def add(i):
            msg = pl.ds(k * h + i, STEP)
            a = sums[pl.ds(2 * h + i, STEP), :] + decode(second_dn[msg, :], dn)
            b = sums[pl.ds(3 * h + i, STEP), :] + decode(second_up[msg, :], up)
            out[pl.ds(pl.multiple_of(first + i, STEP), STEP), :] = a.astype(BF16)
            out[pl.ds(pl.multiple_of(first + h + i, STEP), STEP), :] = b.astype(BF16)

        looped(h, add)


def shape(*dims, dtype=F32):
    return jax.ShapeDtypeStruct(dims, dtype)


def local(inputs, grad_out, weight):
    row, col, dp = (lax.axis_index(n) for n in ("row", "col", "dp"))
    where = jnp.stack([row // 2, row % 2, dp % 2, col]).astype(jnp.int32)
    features, outs = weight.shape
    half = features // 2
    dmas = lambda n: pltpu.SemaphoreType.DMA((n,))

    a = grad_out[0]
    rows = a.shape[0]
    h = rows // 2
    a_dn = lax.ppermute(a, "row", X_UP)
    a_up = lax.ppermute(a, "row", X_DOWN)
    b = lax.ppermute(a, "row", Y_SWAP)
    i_dn = lax.ppermute(inputs[0], "col", Z_UP)
    i_up = lax.ppermute(inputs[0], "col", Z_DOWN)
    far_lo = lax.ppermute(a_up[:h], "row", X_DOWN)
    far_hi = lax.ppermute(a_dn[h:], "row", X_UP)
    b_dn = lax.ppermute(after(b, far_hi), "row", X_UP)
    b_up = lax.ppermute(b, "row", X_DOWN)
    i_far_lo = lax.ppermute(i_up[:rows], "col", Z_DOWN)
    i_far_hi = lax.ppermute(i_dn[rows:], "col", Z_UP)
    b_far_lo = lax.ppermute(far_lo, "row", Y_SWAP)
    b_far_hi = lax.ppermute(far_hi, "row", Y_SWAP)
    side_a, side_b = (a, a_up, far_lo, far_hi, a_dn), (b, b_up, b_far_lo, b_far_hi, b_dn)
    input_pieces = (inputs[0], i_up, i_far_lo, i_far_hi, i_dn)
    tokens = 8 * rows

    spans, first = [], 0
    for width in WIDTHS:
        spans.append((first, width))
        first += width

    last = []

    def ordered(kernel, outs, scratch, specs, *args, **kw):
        results = call(kernel, outs, scratch, [SMEM] + specs, **kw)(after(where, *last), *args)
        last[:] = [results[0]]
        return results

    def terms_of(side, us=0):
        msg = shape(rows + TAIL, features, dtype=BF16)
        up, dn, terms = ordered(
            term_kernel,
            [msg, msg, shape(4, rows, features)],
            [pltpu.VMEM((4, rows, outs), BF16), pltpu.VMEM((features, outs), BF16), dmas(6)],
            [ANY] * 6,
            weight,
            *side,
            mib=22,
            us=us,
        )
        return terms, lax.ppermute(up, "col", Z_UP), lax.ppermute(dn, "col", Z_DOWN)

    def weight_of(j, us=0, parts=None, own=1):
        first, width = spans[j]
        parts = PARTS[j] if parts is None else parts
        got = ordered(
            functools.partial(weight_kernel, first, parts, own),
            [shape(half // max(parts, 1), width)] * parts + [shape(half, width)] * own,
            [pltpu.VMEM((tokens, width), BF16), dmas(20)],
            [VMEM] + [ANY] * 10,
            env["T"],
            *side_a,
            *side_b,
            us=us,
            mib=20,
        )
        return list(got[parts:]) + [lax.ppermute(give, "dp", CORE_SWAP) for give in got[:parts]]

    def pair_of(j, us=0):
        width = spans[j][1]
        parts = env["K%d" % j]
        (msg,) = ordered(
            pair_kernel,
            [shape(half + TAIL, width, dtype=BF16)],
            [pltpu.VMEM((half, width), F32)],
            [VMEM] * len(parts),
            *parts,
            us=us,
        )
        return msg, lax.ppermute(msg, "dp", FAR_SWAP)

    def final_of(j, us=0):
        width = spans[j][1]
        sent, got = env["P%d" % j]
        (mine,) = call(decode_kernel, [shape(half, width)], (), [VMEM])(sent)
        own, n = [], half // HALVES[j]
        for first in range(0, half, n):
            kernel = functools.partial(final_kernel, first)
            own += ordered(kernel, [shape(n, width, dtype=BF16)], (), [VMEM] * 2, mine, got, us=us)
        return own, [lax.ppermute(v, "dp", CORE_SWAP) for v in own]

    def turn(us=0):
        (turned,) = ordered(
            turn_kernel,
            [shape(features, tokens, dtype=BF16)],
            [pltpu.VMEM((tokens, features), BF16), dmas(len(input_pieces))],
            [ANY] * len(input_pieces),
            *input_pieces,
            us=us,
        )
        return turned

    def meet_of(us=0):
        (sums,) = ordered(meet_kernel, [shape(2 * rows, features)], (), [VMEM] * 3, *env["A"], us=us)
        return sums

    def second_of(us=0):
        msg = shape(rows + TAIL, features, dtype=BF16)
        up, dn, sums = ordered(
            second_kernel, [msg, msg, shape(2 * rows, features)], (), [VMEM] * 4, env["M"], *env["B"], mib=18, us=us
        )
        return sums, lax.ppermute(up, "col", Z_UP), lax.ppermute(dn, "col", Z_DOWN)

    def last_of(us=0):
        out = [shape(2 * rows, features, dtype=BF16)]
        (grad_in,) = ordered(last_kernel, out, (), [VMEM] * 4, env["M"], *env["S"], us=us)
        return grad_in

    def place(chunks, sides, us=0):
        old = [env["X"]] if "X" in env else []
        spots, srcs = [], []
        for j in chunks:
            for i in sides:
                for k, src in enumerate(env["F%d" % j][i]):
                    spots.append((spans[j][0], k * src.shape[0], i))
                    srcs.append(src)
        n = len(srcs)
        (out,) = ordered(
            functools.partial(place_kernel, spots),
            [shape(features, outs, dtype=BF16)],
            [dmas(n)],
            [ANY] * (n + len(old)),
            *srcs,
            *old,
            out_specs=[ANY],
            aliases={n + 1: 0} if old else None,
            us=us,
        )
        return out

    def gate(j, us):
        ordered(gate_kernel, [shape(1, dtype=jnp.int32)], (), [ANY], env["P%d" % j][1], out_specs=[SMEM], us=us)

    env = {}
    for name, us in SCHEDULE:
        if name == "A":
            env[name] = terms_of(side_a, us)
        elif name == "B":
            env[name] = terms_of(side_b, us)
        elif name[0] in "XYZ":
            env["X"] = place([int(c) for c in name[1:]], {"X": (0, 1), "Y": (0,), "Z": (1,)}[name[0]], us)
        elif name[0] == "G":
            gate(int(name[1]), us)
        elif name[0] == "H":
            env[name] = weight_of(int(name[1]), us, own=0)
        elif name[0] == "K" and "H" + name[1] in env:
            env[name] = weight_of(int(name[1]), us, parts=0) + env["H" + name[1]]
        elif name[0] in "KPF":
            env[name] = {"K": weight_of, "P": pair_of, "F": final_of}[name[0]](int(name[1]), us)
        else:
            env[name] = {"T": turn, "M": meet_of, "S": second_of, "L": last_of}[name](us)
    grad_in, grad_weight = env["L"], env["X"]
    return (grad_in[None], grad_weight)


def solution(mesh):
    in_specs = (P("dp", "col", "row"), P("dp", "row", "col"), P("row", "col"))
    out_specs = (P("dp", "col", "row"), P("row", "col"))
    return jax.shard_map(local, mesh=mesh, in_specs=in_specs, out_specs=out_specs, check_vma=False)
```

```python
import functools

import jax
import jax.numpy as jnp
from jax import lax
from jax.experimental import pallas as pl
from jax.experimental.pallas import tpu as pltpu
from jax.sharding import PartitionSpec as P

X_UP = [(r, (r + 2) % 8) for r in range(8)]
X_DOWN = [(r, (r - 2) % 8) for r in range(8)]
Y_SWAP = [(r, r ^ 1) for r in range(8)]
Z_UP = [(c, (c + 1) % 4) for c in range(4)]
Z_DOWN = [(c, (c - 1) % 4) for c in range(4)]
CORE_SWAP = [(d, d ^ 1) for d in range(4)]
FAR_SWAP = [(d, d ^ 2) for d in range(4)]

WIDTHS = (1280, 1280)
F32, BF16 = jnp.float32, jnp.bfloat16
ANY = pl.BlockSpec(memory_space=pl.ANY)
VMEM = pl.BlockSpec(memory_space=pltpu.VMEM)
SMEM = pl.BlockSpec(memory_space=pltpu.SMEM)
POWER = 15.0
PARTS = (1, 2)
SCHEDULE = (
    ("A", 0), ("T", 0), ("K0", 6), ("M", 150), ("P0", 0), ("B", 0),
    ("K1", 0), ("P1", 0), ("F0", 0), ("S", 30), ("X0", 0), ("L", 0),
    ("F1", 0), ("Y1", 0), ("Z1", 0),
)
TAIL = 16
STEP = 32


def call(kernel, outs, scratch=(), specs=(), out_specs=None, mib=14, aliases=None, us=0):
    return pl.pallas_call(
        kernel,
        in_specs=list(specs),
        out_specs=out_specs or [VMEM] * len(outs),
        out_shape=list(outs),
        scratch_shapes=list(scratch),
        input_output_aliases=aliases or {},
        compiler_params=pltpu.CompilerParams(vmem_limit_bytes=mib << 20),
        cost_estimate=pl.CostEstimate(flops=1 + us * 10**9, bytes_accessed=1, transcendentals=0),
    )


def after(x, *deps):
    return lax.optimization_barrier((x, *deps))[0]


def encode(srcs, dst):
    c = srcs[0].shape[1]
    m = jnp.zeros((8, c), F32)
    for src in srcs:

        def top_of(i, m, src=src):
            return top_with(m, src[pl.ds(pl.multiple_of(i * STEP, STEP), STEP), :])

        m = lax.fori_loop(0, src.shape[0] // STEP, top_of, m)
    encode_with(m, srcs, dst)


def top_with(m, v):
    return jnp.maximum(m, jnp.max(jnp.abs(v).reshape(STEP // 8, 8, v.shape[1]), axis=0))


def encode_with(m, srcs, dst):
    c = m.shape[1]
    n = sum(src.shape[0] for src in srcs)
    e = jnp.ceil(jnp.log2(jnp.clip(jnp.max(m, keepdims=True), 2.0**-118, 2.0**120)))
    scale = jnp.exp2(8.0 - e)
    first = 0
    for src in srcs:

        @pl.loop(0, src.shape[0] // STEP)
        def _(i, src=src, first=first):
            at = pl.multiple_of(i * STEP, STEP)
            v = src[pl.ds(at, STEP), :] * scale
            v2 = v * v
            v4 = v2 * v2
            code = ((v4 * v4) * v4 * (v2 * v)).astype(BF16)
            for q in range(c // 128):
                dst[pl.ds(q * n + first + at, STEP), :] = code[:, 128 * q : 128 * (q + 1)]

        first += src.shape[0]
    dst[n * c // 128 :, :] = jnp.broadcast_to(e, (TAIL, 128)).astype(BF16)


def message(n, c):
    return jax.ShapeDtypeStruct((n * c // 128 + TAIL, 128), BF16)


def part_of(msg, n, c, i):
    return jnp.concatenate([msg[pl.ds(q * n + i, STEP), :] for q in range(c // 128)], axis=1)


def scale_of(msg):
    n = msg.shape[0] - TAIL
    return jnp.exp2(msg[n:, :].astype(F32)[0:1, 0:1] - 8.0)


def decode(y, scale):
    y = y.astype(F32)
    r = jnp.exp2(jnp.log2(jnp.abs(y)) * (1.0 / POWER)) * scale
    r = jnp.where(y == 0.0, 0.0, r)
    return jnp.where(y < 0.0, -r, r)


def looped(n, body):
    @pl.loop(0, n // STEP)
    def _(i):
        body(pl.multiple_of(i * STEP, STEP))


def turn_kernel(at, *refs):
    pieces, (out, bufs, sems) = refs[:-3], refs[-3:]
    rows = pieces[0].shape[0]
    copies, first = [], 0
    for i, src in enumerate(pieces):
        copies.append(pltpu.make_async_copy(src, bufs.at[pl.ds(first, src.shape[0])], sems.at[i]))
        copies[-1].start()
        first += src.shape[0]
    for copy in copies:
        copy.wait()
    for d in range(4):
        for f in range(0, out.shape[0], 256):
            tokens = pl.ds(pl.multiple_of(lax.rem(at[3] + d, 4) * rows, rows), rows)
            out[f : f + 256, tokens] = bufs[d * rows : (d + 1) * rows, f : f + 256].T


def weight_kernel(first, parts, own, at, inputs, *refs):
    n = 10 + parts + own
    weight_parts(first, at, inputs, refs[:10], refs[10 : 10 + parts], refs[10 + parts : n], *refs[n:])


def weight_parts(first, at, inputs, pieces, gives, keeps, grads, sems):
    x, y, core = at[0], at[1], at[2]
    rows, width = pieces[0].shape[0], grads.shape[1]
    half = inputs.shape[0] // 2
    cut = width // 2 // 256 * 256
    tiles = ((0, cut), (cut, width - cut))
    copies = []
    for t, (column, n) in enumerate(tiles):
        for i, src in enumerate(pieces):
            d, lo = ((0, 0), (1, 0), (2, 0), (2, rows // 2), (3, 0))[i % 5]
            r = 2 * lax.rem(x + d, 4) + lax.rem(y + i // 5, 2)
            start = pl.multiple_of(r * rows + lo, rows // 2)
            dst = grads.at[pl.ds(start, src.shape[0]), pl.ds(column, n)]
            copy = pltpu.make_async_copy(src.at[:, pl.ds(first + column, n)], dst, sems.at[10 * t + i])
            copy.start()
            copies.append(copy)
    wanted = [1 - core] * (len(gives) > 0) + [core] * len(keeps)
    for t, (column, n) in enumerate(tiles):
        for copy in copies[10 * t : 10 * t + 10]:
            copy.wait()
        columns = pl.ds(column, n)
        for i, which in enumerate(wanted):
            features = pl.ds(pl.multiple_of(which * half, half), half)
            value = jnp.dot(inputs[features, :], grads[:, columns], preferred_element_type=F32)
            if i == 0 and gives:
                m = gives[0].shape[0]
                for k, give in enumerate(gives):
                    give[:, columns] = value[k * m : (k + 1) * m]
            else:
                keeps[0][:, columns] = value


def pair_kernel(at, keep, *refs):
    gots, (msg, total) = refs[:-2], refs[-2:]
    n = gots[0].shape[0]
    m = jnp.zeros((8, total.shape[1]), F32)
    for k, got in enumerate(gots):

        def add(i, m, k=k, got=got):
            i = pl.multiple_of(i * STEP, STEP)
            rows = pl.ds(k * n + i, STEP)
            value = keep[rows, :] + got[pl.ds(i, STEP), :]
            total[rows, :] = value
            return top_with(m, value)

        m = lax.fori_loop(0, n // STEP, add, m)
    encode_with(m, [total], msg)


def decode_kernel(msg, out):
    s = scale_of(msg)

    def one(i):
        out[pl.ds(i, STEP), :] = decode(part_of(msg, *out.shape, i), s)

    looped(out.shape[0], one)


def final_kernel(at, mine, got, out):
    s = scale_of(got)

    def add(i):
        rows = pl.ds(i, STEP)
        out[rows, :] = (mine[rows, :] + decode(part_of(got, *out.shape, i), s)).astype(BF16)

    looped(out.shape[0], add)


def place_kernel(spots, at, *refs):
    out, sems = refs[-2:]
    half = out.shape[0] // 2
    copies = []
    for src, (column, row, other) in zip(refs, spots):
        n, width = src.shape
        which = 1 - at[2] if other else at[2]
        rows = pl.ds(pl.multiple_of(which * half + row, n), n)
        copies.append(pltpu.make_async_copy(src, out.at[rows, pl.ds(column, width)], sems.at[len(copies)]))
        copies[-1].start()
    for copy in copies:
        copy.wait()


def gate_kernel(at, got, out):
    out[0] = at[0]


def term_kernel(at, weight, *refs):
    pieces, (up, dn, terms, bufs, held, sems) = refs[:5], refs[5:]
    rows = bufs.shape[1]
    fetch = pltpu.make_async_copy(weight, held, sems.at[5])
    fetch.start()
    copies = []
    for i, (piece, d, lo) in enumerate(zip(pieces, (0, 1, 2, 2, 3), (0, 0, 0, rows // 2, 0))):
        copy = pltpu.make_async_copy(piece, bufs.at[d, pl.ds(lo, piece.shape[0])], sems.at[i])
        copy.start()
        copies.append((copy, d))
    fetch.wait()
    for d in range(4):
        for copy, i in copies:
            if i == d:
                copy.wait()
        s = lax.rem(at[0] + d + 4 - at[3], 4)
        terms[s] = lax.dot_general(bufs[d], held[...], (((1,), (1,)), ((), ())), preferred_element_type=F32)
    h = terms.shape[1] // 2
    lo, hi = pl.ds(0, h), pl.ds(h, h)
    encode([terms.at[2, lo], terms.at[1, hi]], up)
    encode([terms.at[3, lo], terms.at[2, hi]], dn)


def meet(terms, from_dn, from_up, sums):
    h = terms.shape[1] // 2
    n, c = terms.shape[1:]
    dn, up = scale_of(from_dn), scale_of(from_up)

    def add(i):
        lo, hi = pl.ds(i, STEP), pl.ds(h + i, STEP)
        sums[lo, :] = terms[1, lo, :] + decode(part_of(from_dn, n, c, i), dn)
        sums[hi, :] = terms[3, hi, :] + decode(part_of(from_up, n, c, h + i), up)
        sums[pl.ds(2 * h + i, STEP), :] = terms[0, lo, :] + decode(part_of(from_up, n, c, i), up)
        sums[pl.ds(3 * h + i, STEP), :] = terms[0, hi, :] + decode(part_of(from_dn, n, c, h + i), dn)

    looped(h, add)


def meet_kernel(at, terms, from_dn, from_up, sums):
    meet(terms, from_dn, from_up, sums)


def second_kernel(at, sums_a, terms, from_dn, from_up, up, dn, sums_b):
    meet(terms, from_dn, from_up, sums_b)
    h = sums_a.shape[0] // 4
    for first, msg in ((0, up), (h, dn)):
        encode([sums_a.at[pl.ds(first, h)], sums_b.at[pl.ds(first, h)]], msg)


def last_kernel(at, sums_a, sums_b, second_dn, second_up, out):
    dn, up = scale_of(second_dn), scale_of(second_up)
    h, c = sums_a.shape[0] // 4, sums_a.shape[1]
    for k, sums in enumerate((sums_a, sums_b)):
        first = lax.rem(at[1] + k, 2) * (2 * h)

        def add(i):
            a = sums[pl.ds(2 * h + i, STEP), :] + decode(part_of(second_dn, 2 * h, c, k * h + i), dn)
            b = sums[pl.ds(3 * h + i, STEP), :] + decode(part_of(second_up, 2 * h, c, k * h + i), up)
            out[pl.ds(pl.multiple_of(first + i, STEP), STEP), :] = a.astype(BF16)
            out[pl.ds(pl.multiple_of(first + h + i, STEP), STEP), :] = b.astype(BF16)

        looped(h, add)


def shape(*dims, dtype=F32):
    return jax.ShapeDtypeStruct(dims, dtype)


def local(inputs, grad_out, weight):
    row, col, dp = (lax.axis_index(n) for n in ("row", "col", "dp"))
    where = jnp.stack([row // 2, row % 2, dp % 2, col]).astype(jnp.int32)
    features, outs = weight.shape
    half = features // 2
    dmas = lambda n: pltpu.SemaphoreType.DMA((n,))

    a = grad_out[0]
    rows = a.shape[0]
    h = rows // 2
    a_dn = lax.ppermute(a, "row", X_UP)
    a_up = lax.ppermute(a, "row", X_DOWN)
    b = lax.ppermute(a, "row", Y_SWAP)
    i_dn = lax.ppermute(inputs[0], "col", Z_UP)
    i_up = lax.ppermute(inputs[0], "col", Z_DOWN)
    far_lo = lax.ppermute(a_up[:h], "row", X_DOWN)
    far_hi = lax.ppermute(a_dn[h:], "row", X_UP)
    b_dn = lax.ppermute(after(b, far_hi), "row", X_UP)
    b_up = lax.ppermute(b, "row", X_DOWN)
    i_far_lo = lax.ppermute(i_up[:rows], "col", Z_DOWN)
    i_far_hi = lax.ppermute(i_dn[rows:], "col", Z_UP)
    b_far_lo = lax.ppermute(far_lo, "row", Y_SWAP)
    b_far_hi = lax.ppermute(far_hi, "row", Y_SWAP)
    side_a, side_b = (a, a_up, far_lo, far_hi, a_dn), (b, b_up, b_far_lo, b_far_hi, b_dn)
    input_pieces = (inputs[0], i_up, i_far_lo, i_far_hi, i_dn)
    tokens = 8 * rows

    spans, first = [], 0
    for width in WIDTHS:
        spans.append((first, width))
        first += width

    last = []

    def ordered(kernel, outs, scratch, specs, *args, **kw):
        results = call(kernel, outs, scratch, [SMEM] + specs, **kw)(after(where, *last), *args)
        last[:] = [results[0]]
        return results

    def terms_of(side, us=0):
        msg = message(rows, features)
        up, dn, terms = ordered(
            term_kernel,
            [msg, msg, shape(4, rows, features)],
            [pltpu.VMEM((4, rows, outs), BF16), pltpu.VMEM((features, outs), BF16), dmas(6)],
            [ANY] * 6,
            weight,
            *side,
            mib=22,
            us=us,
        )
        return terms, lax.ppermute(up, "col", Z_UP), lax.ppermute(dn, "col", Z_DOWN)

    def weight_of(j, us=0, parts=None, own=1):
        first, width = spans[j]
        parts = PARTS[j] if parts is None else parts
        got = ordered(
            functools.partial(weight_kernel, first, parts, own),
            [shape(half // max(parts, 1), width)] * parts + [shape(half, width)] * own,
            [pltpu.VMEM((tokens, width), BF16), dmas(20)],
            [VMEM] + [ANY] * 10,
            env["T"],
            *side_a,
            *side_b,
            us=us,
            mib=20,
        )
        return list(got[parts:]) + [lax.ppermute(give, "dp", CORE_SWAP) for give in got[:parts]]

    def pair_of(j, us=0):
        width = spans[j][1]
        parts = env["K%d" % j]
        (msg,) = ordered(
            pair_kernel,
            [message(half, width)],
            [pltpu.VMEM((half, width), F32)],
            [VMEM] * len(parts),
            *parts,
            us=us,
        )
        return msg, lax.ppermute(msg, "dp", FAR_SWAP)

    def final_of(j, us=0):
        width = spans[j][1]
        sent, got = env["P%d" % j]
        (mine,) = call(decode_kernel, [shape(half, width)], (), [VMEM])(sent)
        own = ordered(final_kernel, [shape(half, width, dtype=BF16)], (), [VMEM] * 2, mine, got, us=us)
        return list(own), [lax.ppermute(v, "dp", CORE_SWAP) for v in own]

    def turn(us=0):
        (turned,) = ordered(
            turn_kernel,
            [shape(features, tokens, dtype=BF16)],
            [pltpu.VMEM((tokens, features), BF16), dmas(len(input_pieces))],
            [ANY] * len(input_pieces),
            *input_pieces,
            us=us,
        )
        return turned

    def meet_of(us=0):
        (sums,) = ordered(meet_kernel, [shape(2 * rows, features)], (), [VMEM] * 3, *env["A"], us=us)
        return sums

    def second_of(us=0):
        msg = message(rows, features)
        up, dn, sums = ordered(
            second_kernel, [msg, msg, shape(2 * rows, features)], (), [VMEM] * 4, env["M"], *env["B"], mib=18, us=us
        )
        return sums, lax.ppermute(up, "col", Z_UP), lax.ppermute(dn, "col", Z_DOWN)

    def last_of(us=0):
        out = [shape(2 * rows, features, dtype=BF16)]
        (grad_in,) = ordered(last_kernel, out, (), [VMEM] * 4, env["M"], *env["S"], us=us)
        return grad_in

    def place(chunks, sides, us=0):
        old = [env["X"]] if "X" in env else []
        spots, srcs = [], []
        for j in chunks:
            for i in sides:
                for k, src in enumerate(env["F%d" % j][i]):
                    spots.append((spans[j][0], k * src.shape[0], i))
                    srcs.append(src)
        n = len(srcs)
        (out,) = ordered(
            functools.partial(place_kernel, spots),
            [shape(features, outs, dtype=BF16)],
            [dmas(n)],
            [ANY] * (n + len(old)),
            *srcs,
            *old,
            out_specs=[ANY],
            aliases={n + 1: 0} if old else None,
            us=us,
        )
        return out

    def gate(j, us):
        ordered(gate_kernel, [shape(1, dtype=jnp.int32)], (), [ANY], env["P%d" % j][1], out_specs=[SMEM], us=us)

    env = {}
    for name, us in SCHEDULE:
        if name == "A":
            env[name] = terms_of(side_a, us)
        elif name == "B":
            env[name] = terms_of(side_b, us)
        elif name[0] in "XYZ":
            env["X"] = place([int(c) for c in name[1:]], {"X": (0, 1), "Y": (0,), "Z": (1,)}[name[0]], us)
        elif name[0] == "G":
            gate(int(name[1]), us)
        elif name[0] == "H":
            env[name] = weight_of(int(name[1]), us, own=0)
        elif name[0] == "K" and "H" + name[1] in env:
            env[name] = weight_of(int(name[1]), us, parts=0) + env["H" + name[1]]
        elif name[0] in "KPF":
            env[name] = {"K": weight_of, "P": pair_of, "F": final_of}[name[0]](int(name[1]), us)
        else:
            env[name] = {"T": turn, "M": meet_of, "S": second_of, "L": last_of}[name](us)
    grad_in, grad_weight = env["L"], env["X"]
    return (grad_in[None], grad_weight)


def solution(mesh):
    in_specs = (P("dp", "col", "row"), P("dp", "row", "col"), P("row", "col"))
    out_specs = (P("dp", "col", "row"), P("row", "col"))
    return jax.shard_map(local, mesh=mesh, in_specs=in_specs, out_specs=out_specs, check_vma=False)
```

```python
import functools

import jax
import jax.numpy as jnp
from jax import lax
from jax.experimental import pallas as pl
from jax.experimental.pallas import tpu as pltpu
from jax.sharding import PartitionSpec as P

X_UP = [(r, (r + 2) % 8) for r in range(8)]
X_DOWN = [(r, (r - 2) % 8) for r in range(8)]
Y_SWAP = [(r, r ^ 1) for r in range(8)]
Z_UP = [(c, (c + 1) % 4) for c in range(4)]
Z_DOWN = [(c, (c - 1) % 4) for c in range(4)]
CORE_SWAP = [(d, d ^ 1) for d in range(4)]
FAR_SWAP = [(d, d ^ 2) for d in range(4)]

WIDTHS = (1280, 1280)
F32, BF16 = jnp.float32, jnp.bfloat16
ANY = pl.BlockSpec(memory_space=pl.ANY)
VMEM = pl.BlockSpec(memory_space=pltpu.VMEM)
SMEM = pl.BlockSpec(memory_space=pltpu.SMEM)
POWER = 15.0
PARTS = (1, 2)
SCHEDULE = (
    ("A", 0), ("T", 0), ("K0", 6), ("M", 150), ("P0", 0), ("B", 0),
    ("K1", 0), ("P1", 0), ("F0", 0), ("S", 30), ("X0", 0), ("L", 0),
    ("F1", 0), ("Y1", 0), ("Z1", 0),
)
TAIL = 16
ROWS = 160
STEP = 32


def call(kernel, outs, scratch=(), specs=(), out_specs=None, mib=14, aliases=None, us=0):
    return pl.pallas_call(
        kernel,
        in_specs=list(specs),
        out_specs=out_specs or [VMEM] * len(outs),
        out_shape=list(outs),
        scratch_shapes=list(scratch),
        input_output_aliases=aliases or {},
        compiler_params=pltpu.CompilerParams(vmem_limit_bytes=mib << 20),
        cost_estimate=pl.CostEstimate(flops=1 + us * 10**9, bytes_accessed=1, transcendentals=0),
    )


def after(x, *deps):
    return lax.optimization_barrier((x, *deps))[0]


def encode(srcs, dst):
    c = srcs[0].shape[1]
    m = jnp.zeros((8, c), F32)
    for src in srcs:

        def top_of(i, m, src=src):
            return top_with(m, src[pl.ds(pl.multiple_of(i * STEP, STEP), STEP), :])

        m = lax.fori_loop(0, src.shape[0] // STEP, top_of, m)
    encode_with(m, srcs, dst)


def top_with(m, v):
    return jnp.maximum(m, jnp.max(jnp.abs(v).reshape(STEP // 8, 8, v.shape[1]), axis=0))


def encode_with(m, srcs, dst):
    c = m.shape[1]
    n = sum(src.shape[0] for src in srcs)
    e = jnp.ceil(jnp.log2(jnp.clip(jnp.max(m, keepdims=True), 2.0**-118, 2.0**120)))
    scale = jnp.exp2(8.0 - e)
    first = 0
    for src in srcs:

        @pl.loop(0, src.shape[0] // STEP)
        def _(i, src=src, first=first):
            at = pl.multiple_of(i * STEP, STEP)
            v = src[pl.ds(at, STEP), :] * scale
            v2 = v * v
            v4 = v2 * v2
            code = ((v4 * v4) * v4 * (v2 * v)).astype(BF16)
            for q in range(c // 128):
                dst[pl.ds(q * n + first + at, STEP), :] = code[:, 128 * q : 128 * (q + 1)]

        first += src.shape[0]
    dst[n * c // 128 :, :] = jnp.broadcast_to(e, (TAIL, 128)).astype(BF16)


def message(n, c):
    return jax.ShapeDtypeStruct((n * c // 128 + TAIL, 128), BF16)


def part_of(msg, n, c, i):
    return jnp.concatenate([msg[pl.ds(q * n + i, STEP), :] for q in range(c // 128)], axis=1)


def scale_of(msg):
    n = msg.shape[0] - TAIL
    return jnp.exp2(msg[n:, :].astype(F32)[0:1, 0:1] - 8.0)


def decode(y, scale):
    y = y.astype(F32)
    r = jnp.exp2(jnp.log2(jnp.abs(y)) * (1.0 / POWER)) * scale
    r = jnp.where(y == 0.0, 0.0, r)
    return jnp.where(y < 0.0, -r, r)


def looped(n, body):
    @pl.loop(0, n // STEP)
    def _(i):
        body(pl.multiple_of(i * STEP, STEP))


def turn_kernel(at, *refs):
    pieces, (out, bufs, sems) = refs[:-3], refs[-3:]
    rows = pieces[0].shape[0]
    copies, first = [], 0
    for i, src in enumerate(pieces):
        copies.append(pltpu.make_async_copy(src, bufs.at[pl.ds(first, src.shape[0])], sems.at[i]))
        copies[-1].start()
        first += src.shape[0]
    for copy in copies:
        copy.wait()
    for d in range(4):
        for f in range(0, out.shape[0], 256):
            tokens = pl.ds(pl.multiple_of(lax.rem(at[3] + d, 4) * rows, rows), rows)
            out[f : f + 256, tokens] = bufs[d * rows : (d + 1) * rows, f : f + 256].T


def weight_kernel(first, parts, own, at, inputs, *refs):
    n = 10 + parts + own
    weight_parts(first, at, inputs, refs[:10], refs[10 : 10 + parts], refs[10 + parts : n], *refs[n:])


def weight_parts(first, at, inputs, pieces, gives, keeps, grads, sems):
    x, y, core = at[0], at[1], at[2]
    rows, width = pieces[0].shape[0], grads.shape[1]
    half = inputs.shape[0] // 2
    cut = width // 2 // 256 * 256
    tiles = ((0, cut), (cut, width - cut))
    copies = []
    for t, (column, n) in enumerate(tiles):
        for i, src in enumerate(pieces):
            d, lo = ((0, 0), (1, 0), (2, 0), (2, rows // 2), (3, 0))[i % 5]
            r = 2 * lax.rem(x + d, 4) + lax.rem(y + i // 5, 2)
            start = pl.multiple_of(r * rows + lo, rows // 2)
            dst = grads.at[pl.ds(start, src.shape[0]), pl.ds(column, n)]
            copy = pltpu.make_async_copy(src.at[:, pl.ds(first + column, n)], dst, sems.at[10 * t + i])
            copy.start()
            copies.append(copy)
    wanted = [1 - core] * (len(gives) > 0) + [core] * len(keeps)
    for t, (column, n) in enumerate(tiles):
        for copy in copies[10 * t : 10 * t + 10]:
            copy.wait()
        columns = pl.ds(column, n)
        for i, which in enumerate(wanted):
            for k in range(half // ROWS):
                features = pl.ds(pl.multiple_of(which * half + k * ROWS, ROWS), ROWS)
                value = jnp.dot(inputs[features, :], grads[:, columns], preferred_element_type=F32)
                if i == 0 and gives:
                    m = gives[0].shape[0]
                    gives[k * ROWS // m][pl.ds(k * ROWS % m, ROWS), columns] = value
                else:
                    keeps[0][pl.ds(k * ROWS, ROWS), columns] = value


def pair_kernel(at, keep, *refs):
    gots, (msg, total) = refs[:-2], refs[-2:]
    n = gots[0].shape[0]
    m = jnp.zeros((8, total.shape[1]), F32)
    for k, got in enumerate(gots):

        def add(i, m, k=k, got=got):
            i = pl.multiple_of(i * STEP, STEP)
            rows = pl.ds(k * n + i, STEP)
            value = keep[rows, :] + got[pl.ds(i, STEP), :]
            total[rows, :] = value
            return top_with(m, value)

        m = lax.fori_loop(0, n // STEP, add, m)
    encode_with(m, [total], msg)


def decode_kernel(msg, out):
    s = scale_of(msg)

    def one(i):
        out[pl.ds(i, STEP), :] = decode(part_of(msg, *out.shape, i), s)

    looped(out.shape[0], one)


def final_kernel(at, mine, got, out):
    s = scale_of(got)

    def add(i):
        rows = pl.ds(i, STEP)
        out[rows, :] = (mine[rows, :] + decode(part_of(got, *out.shape, i), s)).astype(BF16)

    looped(out.shape[0], add)


def place_kernel(spots, at, *refs):
    out, sems = refs[-2:]
    half = out.shape[0] // 2
    copies = []
    for src, (column, row, other) in zip(refs, spots):
        n, width = src.shape
        which = 1 - at[2] if other else at[2]
        rows = pl.ds(pl.multiple_of(which * half + row, n), n)
        copies.append(pltpu.make_async_copy(src, out.at[rows, pl.ds(column, width)], sems.at[len(copies)]))
        copies[-1].start()
    for copy in copies:
        copy.wait()


def gate_kernel(at, got, out):
    out[0] = at[0]


def term_kernel(at, weight, *refs):
    pieces, (up, dn, terms, bufs, held, sems) = refs[:5], refs[5:]
    rows = bufs.shape[1]
    fetch = pltpu.make_async_copy(weight, held, sems.at[5])
    fetch.start()
    copies = []
    for i, (piece, d, lo) in enumerate(zip(pieces, (0, 1, 2, 2, 3), (0, 0, 0, rows // 2, 0))):
        copy = pltpu.make_async_copy(piece, bufs.at[d, pl.ds(lo, piece.shape[0])], sems.at[i])
        copy.start()
        copies.append((copy, d))
    fetch.wait()
    for d in range(4):
        for copy, i in copies:
            if i == d:
                copy.wait()
        s = lax.rem(at[0] + d + 4 - at[3], 4)
        terms[s] = lax.dot_general(bufs[d], held[...], (((1,), (1,)), ((), ())), preferred_element_type=F32)
    h = terms.shape[1] // 2
    lo, hi = pl.ds(0, h), pl.ds(h, h)
    encode([terms.at[2, lo], terms.at[1, hi]], up)
    encode([terms.at[3, lo], terms.at[2, hi]], dn)


def meet(terms, from_dn, from_up, sums):
    h = terms.shape[1] // 2
    n, c = terms.shape[1:]
    dn, up = scale_of(from_dn), scale_of(from_up)

    def add(i):
        lo, hi = pl.ds(i, STEP), pl.ds(h + i, STEP)
        sums[lo, :] = terms[1, lo, :] + decode(part_of(from_dn, n, c, i), dn)
        sums[hi, :] = terms[3, hi, :] + decode(part_of(from_up, n, c, h + i), up)
        sums[pl.ds(2 * h + i, STEP), :] = terms[0, lo, :] + decode(part_of(from_up, n, c, i), up)
        sums[pl.ds(3 * h + i, STEP), :] = terms[0, hi, :] + decode(part_of(from_dn, n, c, h + i), dn)

    looped(h, add)


def meet_kernel(at, terms, from_dn, from_up, sums):
    meet(terms, from_dn, from_up, sums)


def second_kernel(at, sums_a, terms, from_dn, from_up, up, dn, sums_b):
    meet(terms, from_dn, from_up, sums_b)
    h = sums_a.shape[0] // 4
    for first, msg in ((0, up), (h, dn)):
        encode([sums_a.at[pl.ds(first, h)], sums_b.at[pl.ds(first, h)]], msg)


def last_kernel(at, sums_a, sums_b, second_dn, second_up, out):
    dn, up = scale_of(second_dn), scale_of(second_up)
    h, c = sums_a.shape[0] // 4, sums_a.shape[1]
    for k, sums in enumerate((sums_a, sums_b)):
        first = lax.rem(at[1] + k, 2) * (2 * h)

        def add(i):
            a = sums[pl.ds(2 * h + i, STEP), :] + decode(part_of(second_dn, 2 * h, c, k * h + i), dn)
            b = sums[pl.ds(3 * h + i, STEP), :] + decode(part_of(second_up, 2 * h, c, k * h + i), up)
            out[pl.ds(pl.multiple_of(first + i, STEP), STEP), :] = a.astype(BF16)
            out[pl.ds(pl.multiple_of(first + h + i, STEP), STEP), :] = b.astype(BF16)

        looped(h, add)


def shape(*dims, dtype=F32):
    return jax.ShapeDtypeStruct(dims, dtype)


def local(inputs, grad_out, weight):
    row, col, dp = (lax.axis_index(n) for n in ("row", "col", "dp"))
    where = jnp.stack([row // 2, row % 2, dp % 2, col]).astype(jnp.int32)
    features, outs = weight.shape
    half = features // 2
    dmas = lambda n: pltpu.SemaphoreType.DMA((n,))

    a = grad_out[0]
    rows = a.shape[0]
    h = rows // 2
    a_dn = lax.ppermute(a, "row", X_UP)
    a_up = lax.ppermute(a, "row", X_DOWN)
    b = lax.ppermute(a, "row", Y_SWAP)
    i_dn = lax.ppermute(inputs[0], "col", Z_UP)
    i_up = lax.ppermute(inputs[0], "col", Z_DOWN)
    far_lo = lax.ppermute(a_up[:h], "row", X_DOWN)
    far_hi = lax.ppermute(a_dn[h:], "row", X_UP)
    b_dn = lax.ppermute(after(b, far_hi), "row", X_UP)
    b_up = lax.ppermute(b, "row", X_DOWN)
    i_far_lo = lax.ppermute(i_up[:rows], "col", Z_DOWN)
    i_far_hi = lax.ppermute(i_dn[rows:], "col", Z_UP)
    b_far_lo = lax.ppermute(far_lo, "row", Y_SWAP)
    b_far_hi = lax.ppermute(far_hi, "row", Y_SWAP)
    side_a, side_b = (a, a_up, far_lo, far_hi, a_dn), (b, b_up, b_far_lo, b_far_hi, b_dn)
    input_pieces = (inputs[0], i_up, i_far_lo, i_far_hi, i_dn)
    tokens = 8 * rows

    spans, first = [], 0
    for width in WIDTHS:
        spans.append((first, width))
        first += width

    last = []

    def ordered(kernel, outs, scratch, specs, *args, **kw):
        results = call(kernel, outs, scratch, [SMEM] + specs, **kw)(after(where, *last), *args)
        last[:] = [results[0]]
        return results

    def terms_of(side, us=0):
        msg = message(rows, features)
        up, dn, terms = ordered(
            term_kernel,
            [msg, msg, shape(4, rows, features)],
            [pltpu.VMEM((4, rows, outs), BF16), pltpu.VMEM((features, outs), BF16), dmas(6)],
            [ANY] * 6,
            weight,
            *side,
            mib=22,
            us=us,
        )
        return terms, lax.ppermute(up, "col", Z_UP), lax.ppermute(dn, "col", Z_DOWN)

    def weight_of(j, us=0, parts=None, own=1):
        first, width = spans[j]
        parts = PARTS[j] if parts is None else parts
        got = ordered(
            functools.partial(weight_kernel, first, parts, own),
            [shape(half // max(parts, 1), width)] * parts + [shape(half, width)] * own,
            [pltpu.VMEM((tokens, width), BF16), dmas(20)],
            [VMEM] + [ANY] * 10,
            env["T"],
            *side_a,
            *side_b,
            us=us,
            mib=20,
        )
        return list(got[parts:]) + [lax.ppermute(give, "dp", CORE_SWAP) for give in got[:parts]]

    def pair_of(j, us=0):
        width = spans[j][1]
        parts = env["K%d" % j]
        (msg,) = ordered(
            pair_kernel,
            [message(half, width)],
            [pltpu.VMEM((half, width), F32)],
            [VMEM] * len(parts),
            *parts,
            us=us,
        )
        return msg, lax.ppermute(msg, "dp", FAR_SWAP)

    def final_of(j, us=0):
        width = spans[j][1]
        sent, got = env["P%d" % j]
        (mine,) = call(decode_kernel, [shape(half, width)], (), [VMEM])(sent)
        own = ordered(final_kernel, [shape(half, width, dtype=BF16)], (), [VMEM] * 2, mine, got, us=us)
        return list(own), [lax.ppermute(v, "dp", CORE_SWAP) for v in own]

    def turn(us=0):
        (turned,) = ordered(
            turn_kernel,
            [shape(features, tokens, dtype=BF16)],
            [pltpu.VMEM((tokens, features), BF16), dmas(len(input_pieces))],
            [ANY] * len(input_pieces),
            *input_pieces,
            us=us,
        )
        return turned

    def meet_of(us=0):
        (sums,) = ordered(meet_kernel, [shape(2 * rows, features)], (), [VMEM] * 3, *env["A"], us=us)
        return sums

    def second_of(us=0):
        msg = message(rows, features)
        up, dn, sums = ordered(
            second_kernel, [msg, msg, shape(2 * rows, features)], (), [VMEM] * 4, env["M"], *env["B"], mib=18, us=us
        )
        return sums, lax.ppermute(up, "col", Z_UP), lax.ppermute(dn, "col", Z_DOWN)

    def last_of(us=0):
        out = [shape(2 * rows, features, dtype=BF16)]
        (grad_in,) = ordered(last_kernel, out, (), [VMEM] * 4, env["M"], *env["S"], us=us)
        return grad_in

    def place(chunks, sides, us=0):
        old = [env["X"]] if "X" in env else []
        spots, srcs = [], []
        for j in chunks:
            for i in sides:
                for k, src in enumerate(env["F%d" % j][i]):
                    spots.append((spans[j][0], k * src.shape[0], i))
                    srcs.append(src)
        n = len(srcs)
        (out,) = ordered(
            functools.partial(place_kernel, spots),
            [shape(features, outs, dtype=BF16)],
            [dmas(n)],
            [ANY] * (n + len(old)),
            *srcs,
            *old,
            out_specs=[ANY],
            aliases={n + 1: 0} if old else None,
            us=us,
        )
        return out

    def gate(j, us):
        ordered(gate_kernel, [shape(1, dtype=jnp.int32)], (), [ANY], env["P%d" % j][1], out_specs=[SMEM], us=us)

    env = {}
    for name, us in SCHEDULE:
        if name == "A":
            env[name] = terms_of(side_a, us)
        elif name == "B":
            env[name] = terms_of(side_b, us)
        elif name[0] in "XYZ":
            env["X"] = place([int(c) for c in name[1:]], {"X": (0, 1), "Y": (0,), "Z": (1,)}[name[0]], us)
        elif name[0] == "G":
            gate(int(name[1]), us)
        elif name[0] == "H":
            env[name] = weight_of(int(name[1]), us, own=0)
        elif name[0] == "K" and "H" + name[1] in env:
            env[name] = weight_of(int(name[1]), us, parts=0) + env["H" + name[1]]
        elif name[0] in "KPF":
            env[name] = {"K": weight_of, "P": pair_of, "F": final_of}[name[0]](int(name[1]), us)
        else:
            env[name] = {"T": turn, "M": meet_of, "S": second_of, "L": last_of}[name](us)
    grad_in, grad_weight = env["L"], env["X"]
    return (grad_in[None], grad_weight)


def solution(mesh):
    in_specs = (P("dp", "col", "row"), P("dp", "row", "col"), P("row", "col"))
    out_specs = (P("dp", "col", "row"), P("row", "col"))
    return jax.shard_map(local, mesh=mesh, in_specs=in_specs, out_specs=out_specs, check_vma=False)
```
